32 devices in a mesh: half: 2 (over core), row: 4 (over y, x), col: 4 (over z).
Axes of the slice: x: 2, y: 2, z: 4, core: 2. Of those that a mesh axis runs over, the one named last changes fastest.
Arguments:
- child_diag: float32 [2, 512, 512], P('half'), as said below
- child_panel: float32 [2, 32, 4, 128, 512], P('half', None, 'row'), may hold values from -18 to 18
- child_window: float32 [2, 32, 4, 128, 16, 4, 128], P('half', None, 'row', None, None, 'col'), may hold values from -6 to 6
- parent_diag: float32 [512, 512], replicated
- parent_lead_panel: float32 [48, 4, 2, 4, 16, 512], P(None, 'row', 'half', 'col'), may hold values from -24 to 24
- index_maps: int32 [2, 128], replicated, may hold values from 0 to 191, as said below
Outputs:
- parent_front: float32 [48, 4, 128, 8, 2, 4, 128], P(None, 'row', None, None, 'half', 'col')
- parent_factor: float32 [48, 4, 2, 4, 16, 512], P(None, 'row', 'half', 'col')
- parent_pivot: float32 [512, 512], replicated
The draws below stay inside these ranges and needn't reach their ends.
Inputs may be any that keep to these rules, and one draw needn't show every extreme that they name: child_diag and parent_diag are symmetric and positive definite. For each child k and each group a, the entries index_maps[k, a * 8 + u] with 0 <= u < 8 equal q * 8 + ((u + s) mod 8) for a group target q and a turn s fixed within the group; groups a < 8 have q = a, later groups have distinct q that rise with a; over the 8 groups of a child the turns s, taken modulo 8, are all different; for each child some group a < 8 has a turn divisible by 8, and another group a < 8 has a turn that leaves 1 modulo 8.
All inputs are finite; a program needn't handle non-finite values.
Results may differ from the reference program's by a relative error of at most 0.0001.
Values sent between devices are 32-bit elements; how exact they have to be, the bound alone decides.
A program may use at most 256 MiB of HBM per device.

```python
import jax
import jax.numpy as jnp
from jax import lax

BLOCK_EXTENT = 128
PANEL_COLUMNS = 512
SB = 128
RB = 192
WB = 64
GRP = 8
NG = 16
WG = 8
PGR = 24
SBL = 32
WLC = 16
PARENT_ROWS = 48
PARENT_COLUMNS = 8
PANEL_SUBROWS = 16
N_HALF = 2
N_ROW = 4
N_COL = 4


def spd_blocks(base_key, block_count):
    random_key, pivot_key, lead_key, side_key = jax.random.split(base_key, 4)
    shape = (block_count, PANEL_COLUMNS, PANEL_COLUMNS)
    random_part = jax.random.uniform(random_key, shape, jnp.float32, -1.0, 1.0)
    lead = jax.random.uniform(lead_key, (block_count, PANEL_COLUMNS), jnp.float32, 1.5, 2.5)
    side = jax.random.uniform(side_key, (block_count, PANEL_COLUMNS), jnp.float32, -1.5, 1.5)
    mirror = 0.5 * (random_part + jnp.swapaxes(random_part, 1, 2))
    pivots = jax.random.uniform(pivot_key, (block_count, PANEL_COLUMNS), jnp.float32, 1.2 * PANEL_COLUMNS, 2.4 * PANEL_COLUMNS)
    identity = jnp.eye(PANEL_COLUMNS, dtype=jnp.float32)
    coupling = lead[:, :, None] * lead[:, None, :] + side[:, :, None] * side[:, None, :]
    return mirror * (1.0 - identity) + identity * pivots[:, :, None] + coupling


def draw_child_diag(key, part):
    return spd_blocks(jax.random.fold_in(key, 3), 2)


def draw_parent_diag(key, part):
    return spd_blocks(jax.random.fold_in(key, 5), 1)[0]


def draw_index_maps(key, part):
    row_count = GRP // 2
    run_count = NG // row_count
    leading_count = min(WG, row_count)
    chosen = []
    for child_id in range(2):
        child_key = jax.random.fold_in(key, 11 + child_id)
        perm_key, bit_key, group_key = jax.random.split(child_key, 3)
        pick_key = jax.random.fold_in(child_key, 29)
        order_key = jax.random.fold_in(child_key, 31)
        runs = jax.vmap(lambda sub_key: jax.random.permutation(sub_key, row_count))(jax.random.split(perm_key, run_count)).astype(jnp.int32)
        leading = jax.random.permutation(pick_key, leading_count)[:2].astype(jnp.int32)
        shuffled = jax.random.permutation(order_key, row_count).astype(jnp.int32)
        keep = jnp.all(shuffled[:, None] != leading[None, :], axis=1)
        others = shuffled[jnp.nonzero(keep, size=row_count - 2)[0]]
        order = jnp.concatenate([leading, others])
        first_run = jnp.zeros((row_count,), jnp.int32).at[order].set(jnp.arange(row_count, dtype=jnp.int32))
        residues = runs.at[0].set(first_run).reshape(NG)
        half_bits = jax.random.randint(bit_key, (NG,), 0, 2)
        shifts = residues + row_count * half_bits
        shuffled_groups = jax.random.permutation(group_key, PGR - 1 - WG)
        later_groups = jnp.nonzero(shuffled_groups < NG - WG - 1, size=NG - WG - 1)[0] + WG
        targets = jnp.concatenate([jnp.arange(WG), later_groups, jnp.array([PGR - 1])])
        offsets = jnp.arange(GRP)
        blocks = GRP * targets[:, None] + (offsets[None, :] + shifts[:, None]) % GRP
        chosen.append(blocks.reshape(SB))
    return jnp.stack(chosen).astype(jnp.int32)


def shard_levels(key, dims, shards, least, high):
    def one(position, shards_of):
        steps = jax.random.uniform(jax.random.fold_in(jax.random.fold_in(key, 6), position), (shards_of,), jnp.float32, least / len(shards), high / len(shards))
        return jnp.repeat(jnp.exp(steps), dims[position] // shards_of).reshape((-1,) + (1,) * (len(dims) - position - 1))

    factor_of = one(*shards[0])
    for cut in shards[1:]:
        factor_of = factor_of * one(*cut)
    return factor_of


def centred(key, dims, spread, most, shards=(), kind=jnp.bfloat16):
    factor_of = shard_levels(key, dims, shards, -0.22, 0.18) if shards else 1.0
    values = jax.random.normal(key, dims, jnp.float32) * spread * factor_of
    return jnp.minimum(jnp.maximum(values, -most), most).astype(kind)


def setup_inputs(seed: int = 0) -> dict:
    key_of = jax.random.split(jax.random.key(seed), 7)
    child_diag = draw_child_diag(jax.random.fold_in(key_of[6], 71), 0)
    child_panel = centred(key_of[1], (2, SBL, N_ROW, BLOCK_EXTENT, PANEL_COLUMNS), 3.0, 18.0, ((0, 2), (2, 4)), jnp.float32)
    child_window = centred(key_of[2], (2, SBL, N_ROW, BLOCK_EXTENT, WLC, N_COL, BLOCK_EXTENT), 1.0, 6.0, ((0, 2), (2, 4), (5, 4)), jnp.float32)
    parent_diag = draw_parent_diag(jax.random.fold_in(key_of[6], 71), 0)
    parent_lead_panel = centred(key_of[4], (PARENT_ROWS, N_ROW, N_HALF, N_COL, PANEL_SUBROWS, PANEL_COLUMNS), 4.0, 24.0, ((1, 4), (2, 2), (3, 4)), jnp.float32)
    index_maps = draw_index_maps(jax.random.fold_in(key_of[6], 71), 0)
    return {"child_diag": child_diag, "child_panel": child_panel, "child_window": child_window, "parent_diag": parent_diag, "parent_lead_panel": parent_lead_panel, "index_maps": index_maps}


def right_solve(factor_low, row_block):
    return jax.scipy.linalg.solve_triangular(factor_low, row_block.T, lower=True).T

def reference(child_diag, child_panel, child_window, parent_diag, parent_lead_panel, index_maps):
    highest = lax.Precision.HIGHEST
    columns = WB * BLOCK_EXTENT
    pivot_lower_factor = jnp.linalg.cholesky(parent_diag)
    parent_row_blocks = right_solve(pivot_lower_factor, parent_lead_panel.reshape(RB * BLOCK_EXTENT, PANEL_COLUMNS))
    assembled_front = jnp.zeros((RB * BLOCK_EXTENT, columns), jnp.float32)
    inside = jnp.arange(BLOCK_EXTENT, dtype=jnp.int32)
    for child_id in range(2):
        child_low = jnp.linalg.cholesky(child_diag[child_id])
        child_rows = right_solve(child_low, child_panel[child_id].reshape(SB * BLOCK_EXTENT, PANEL_COLUMNS))
        schur_part = child_window[child_id].reshape(SB * BLOCK_EXTENT, columns) - jnp.dot(child_rows, child_rows[:columns].T, precision=highest)
        row_index = (index_maps[child_id][:, None] * BLOCK_EXTENT + inside[None, :]).reshape(SB * BLOCK_EXTENT).astype(jnp.int32)
        assembled_front = assembled_front.at[row_index[:, None], row_index[None, :columns]].add(schur_part)
    assembled_front = assembled_front - jnp.dot(parent_row_blocks, parent_row_blocks[:columns].T, precision=highest)
    return (assembled_front.reshape(PARENT_ROWS, N_ROW, BLOCK_EXTENT, PARENT_COLUMNS, N_HALF, N_COL, BLOCK_EXTENT), parent_row_blocks.reshape(PARENT_ROWS, N_ROW, N_HALF, N_COL, PANEL_SUBROWS, PANEL_COLUMNS), pivot_lower_factor)
```

```python
import jax
import jax.numpy as jnp
from jax import lax
from jax.experimental import pallas as pl
from jax.experimental.pallas import tpu as pltpu
from jax.sharding import PartitionSpec as P

EXTENT = 128
VMEM_BYTES = 48 * 1024 * 1024


def from_root(shard, axis, root):
    mine = lax.axis_index(axis) == root
    return lax.psum(jnp.where(mine, shard, jnp.zeros_like(shard)), axis)


def rank_among(first, second):
    size = first.shape[-1]
    before = jnp.arange(size)[None, :] < jnp.arange(size)[:, None]
    same = (first[..., :, None] == first[..., None, :]) & (second[..., :, None] == second[..., None, :])
    return jnp.sum((same & before).astype(jnp.int32), axis=-1)


def pack_kernel(row_to, row_slot, col_half, col_col, col_slot, w_ref, o_ref):
    count = col_half.shape[0]
    for j in range(count):
        o_ref[col_half[j], 0, col_col[j], 0, col_slot[j]] = w_ref[0, pl.ds(j, EXTENT, stride=count), :]


def pack(window, row_to, row_slot, col_half, col_col, col_slot, row_size, per_row, per_col):
    row_local, span, _ = window.shape
    block = (2, 1, row_size, 1, per_col, EXTENT, EXTENT)
    return pl.pallas_call(
        pack_kernel,
        out_shape=jax.ShapeDtypeStruct((2, row_size, row_size, per_row, per_col, EXTENT, EXTENT), jnp.float32),
        grid_spec=pltpu.PrefetchScalarGridSpec(
            num_scalar_prefetch=5,
            grid=(row_local,),
            in_specs=[pl.BlockSpec((1, span, EXTENT), lambda i, *_: (i, 0, 0))],
            out_specs=pl.BlockSpec(block, lambda i, to, slot, *_: (0, to[i], 0, slot[i], 0, 0, 0)),
        ),
        compiler_params=pltpu.CompilerParams(vmem_limit_bytes=VMEM_BYTES),
        cost_estimate=pl.CostEstimate(flops=0, bytes_accessed=8 * window.size, transcendentals=0),
        name="pack",
    )(row_to, row_slot, col_half, col_col, col_slot, window)


def split(value):
    high = value.astype(jnp.bfloat16)
    return high, (value - high.astype(jnp.float32)).astype(jnp.bfloat16)


def times_transpose(left, right):
    return lax.dot_general(left, right, (((1,), (1,)), ((), ())), preferred_element_type=jnp.float32)


def update_kernel(source, slot, present, f0_ref, f1_ref, p_ref, b_ref, o_ref, high, low):
    step = pl.program_id(0)

    @pl.when(step == 0)
    def _():
        for part in range(3):
            high[part], low[part] = split(b_ref[part])

    def product(value, part):
        a_high, a_low = split(value)
        return (
            times_transpose(a_low, high[part])
            + times_transpose(a_high, low[part])
            + times_transpose(a_high, high[part])
        )

    o_ref[0] = -product(p_ref[0], 2)
    for child, ref in enumerate((f0_ref, f1_ref)):

        @pl.when(present[child, step] > 0)
        def _(ref=ref, child=child):
            o_ref[0] -= product(ref[0, 0, 0], child)


def update(factors, parent, columns, source, slot, present):
    rows, _, width = parent.shape
    span = columns.shape[1]
    f_block = (1, 1, 1, EXTENT, width)
    return pl.pallas_call(
        update_kernel,
        out_shape=jax.ShapeDtypeStruct((rows, EXTENT, span), jnp.float32),
        grid_spec=pltpu.PrefetchScalarGridSpec(
            num_scalar_prefetch=3,
            grid=(rows,),
            in_specs=[
                pl.BlockSpec(f_block, lambda i, a, b, c: (0, a[0, i], b[0, i], 0, 0)),
                pl.BlockSpec(f_block, lambda i, a, b, c: (1, a[1, i], b[1, i], 0, 0)),
                pl.BlockSpec((1, EXTENT, width), lambda i, *_: (i, 0, 0)),
                pl.BlockSpec((3, span, width), lambda i, *_: (0, 0, 0)),
            ],
            out_specs=pl.BlockSpec((1, EXTENT, span), lambda i, *_: (i, 0, 0)),
            scratch_shapes=[pltpu.VMEM((3, span, width), jnp.bfloat16)] * 2,
        ),
        compiler_params=pltpu.CompilerParams(vmem_limit_bytes=VMEM_BYTES),
        cost_estimate=pl.CostEstimate(
            flops=18 * rows * EXTENT * span * width, bytes_accessed=16 * rows * EXTENT * width, transcendentals=0
        ),
        name="update",
    )(source, slot, present, factors, factors, parent, columns)


def add_kernel(source, slot, present, col_from, col_slot, w0_ref, w1_ref, u_ref, o_ref):
    step = pl.program_id(0)
    count = o_ref.shape[1] // EXTENT
    for q in range(count):
        value = u_ref[0, :, q * EXTENT : (q + 1) * EXTENT]
        for child, ref in enumerate((w0_ref, w1_ref)):
            block = ref[0, 0, col_from[child, q], 0, col_slot[child, q]]
            value += jnp.where(present[child, step] > 0, block, 0.0)
        o_ref[0, pl.ds(q, EXTENT, stride=count), :] = value


def add_blocks(arrived, updates, source, slot, present, col_from, col_slot):
    _, row_size, _, per_row, per_col, _, _ = arrived.shape
    rows, _, span = updates.shape
    w_block = (1, 1, row_size, 1, per_col, EXTENT, EXTENT)
    return pl.pallas_call(
        add_kernel,
        out_shape=jax.ShapeDtypeStruct((rows, span, EXTENT), jnp.float32),
        grid_spec=pltpu.PrefetchScalarGridSpec(
            num_scalar_prefetch=5,
            grid=(rows,),
            in_specs=[
                pl.BlockSpec(w_block, lambda i, a, b, *_: (0, a[0, i], 0, b[0, i], 0, 0, 0)),
                pl.BlockSpec(w_block, lambda i, a, b, *_: (1, a[1, i], 0, b[1, i], 0, 0, 0)),
                pl.BlockSpec((1, EXTENT, span), lambda i, *_: (i, 0, 0)),
            ],
            out_specs=pl.BlockSpec((1, span, EXTENT), lambda i, *_: (i, 0, 0)),
        ),
        compiler_params=pltpu.CompilerParams(vmem_limit_bytes=VMEM_BYTES),
        cost_estimate=pl.CostEstimate(
            flops=2 * updates.size, bytes_accessed=16 * updates.size, transcendentals=0
        ),
        name="add_blocks",
    )(source, slot, present, col_from, col_slot, arrived, arrived, updates)


def per_device(child_diag, child_panel, child_window, parent_diag, parent_lead_panel, index_maps):
    row_size = lax.axis_size("row")
    half_id = lax.axis_index("half")
    row_id = lax.axis_index("row")
    col_id = lax.axis_index("col")
    group = 2 * row_size
    row_local = child_window.shape[1]
    col_local = child_window.shape[4]
    width = child_panel.shape[-1]
    sub_rows = parent_lead_panel.shape[4]
    parent_rows = parent_lead_panel.shape[0]
    blocks = row_local * row_size
    lead = col_local * row_size
    parent_cols = lead // group
    per_row = 2 * (blocks // group) // row_size
    per_col = (lead // group + row_size - 1) // row_size

    lead_maps = index_maps[:, :lead]
    dealt = jnp.broadcast_to(jnp.arange(blocks, dtype=jnp.int32) % row_size, index_maps.shape)
    row_ranks = rank_among(index_maps % row_size, dealt)
    col_ranks = rank_among(lead_maps % group, dealt[:, :lead])

    def held(values, axis_id):
        mine = lax.dynamic_index_in_dim(values, half_id, axis=0, keepdims=False)
        return lax.dynamic_index_in_dim(mine.reshape(-1, row_size), axis_id, axis=1, keepdims=False)

    row_to = held(index_maps % row_size, row_id)
    row_slot = held(row_ranks, row_id)
    col_to = held(lead_maps % group, col_id)
    col_slot = held(col_ranks, col_id)
    outgoing = pack(
        child_window.reshape(row_local, EXTENT * col_local, EXTENT),
        row_to,
        row_slot,
        col_to // row_size,
        col_to % row_size,
        col_slot,
        row_size,
        per_row,
        per_col,
    )
    arrived = lax.all_to_all(
        outgoing.reshape(-1, per_row * per_col, EXTENT, EXTENT),
        ("half", "row", "col"),
        split_axis=0,
        concat_axis=0,
        tiled=True,
    ).reshape(outgoing.shape)

    gathered = lax.all_gather(
        parent_lead_panel.reshape(parent_rows, sub_rows, width), ("half", "col"), axis=1, tiled=True
    )
    paired = gathered[: 2 * parent_cols].reshape(parent_cols, 2, EXTENT, width)
    offered = lax.dynamic_index_in_dim(paired, half_id, axis=1, keepdims=False)
    column_panel = from_root(offered, "row", col_id)

    child_low = jnp.linalg.cholesky(child_diag[0])
    child_rows = child_panel.reshape(-1, width)
    child_factor = jax.scipy.linalg.solve_triangular(child_low, child_rows.T, lower=True).T
    child_blocks = child_factor.reshape(row_local, EXTENT, width)
    own = jnp.arange(row_local, dtype=jnp.int32)
    row_pick = (row_to == jnp.arange(row_size)[:, None, None]) & (row_slot == jnp.arange(per_row)[:, None])
    row_list = jnp.sum(jnp.where(row_pick, own, 0), axis=-1)
    wanted = jnp.arange(2)[:, None, None] * row_size + col_id
    col_pick = (held(lead_maps % group, row_id) == wanted) & (
        held(col_ranks, row_id) == jnp.arange(per_col)[:, None]
    )
    col_list = jnp.sum(jnp.where(col_pick, own[:col_local], 0), axis=-1)
    picked = jnp.concatenate(
        [
            jnp.broadcast_to(row_list[None], (2, row_size, per_row)),
            jnp.broadcast_to(col_list[:, None], (2, row_size, per_col)),
        ],
        axis=-1,
    )
    exchanged = lax.all_to_all(
        jnp.take(child_blocks, picked.reshape(group, -1), axis=0, mode="clip"),
        ("half", "row"),
        split_axis=0,
        concat_axis=0,
        tiled=True,
    ).reshape(2, row_size, per_row + per_col, EXTENT, width)

    pivot = jnp.linalg.cholesky(parent_diag)
    both = jnp.concatenate([gathered.reshape(-1, width), column_panel.reshape(-1, width)], axis=0)
    solved = jax.scipy.linalg.solve_triangular(pivot, both.T, lower=True).T
    parent = solved[: parent_rows * EXTENT].reshape(parent_rows, EXTENT, width)
    parent_columns = solved[parent_rows * EXTENT :]
    parent_factor = lax.dynamic_slice_in_dim(
        parent, (half_id * row_size + col_id) * sub_rows, sub_rows, axis=1
    )

    ids = jnp.arange(blocks, dtype=jnp.int32)
    row_match = index_maps[:, None, :] == (jnp.arange(parent_rows) * row_size + row_id)[:, None]
    present = jnp.any(row_match, axis=-1).astype(jnp.int32)
    row_from = jnp.sum(jnp.where(row_match, ids % row_size, 0), axis=-1)
    row_from_slot = jnp.sum(jnp.where(row_match, row_ranks[:, None, :], 0), axis=-1)
    targets = jnp.arange(parent_cols) * group + half_id * row_size + col_id
    col_match = lead_maps[:, None, :] == targets[:, None]
    col_from = jnp.sum(jnp.where(col_match, ids[:lead] % row_size, 0), axis=-1)
    col_from_slot = jnp.sum(jnp.where(col_match, col_ranks[:, None, :], 0), axis=-1)

    child_ids = jnp.arange(2)[:, None]
    child_columns = exchanged[child_ids, col_from, per_row + col_from_slot]
    columns = jnp.concatenate(
        [child_columns.reshape(2, -1, width), parent_columns[None]], axis=0
    )
    updates = update(exchanged, parent, columns, row_from, row_from_slot, present)
    front = add_blocks(arrived, updates, row_from, row_from_slot, present, col_from, col_from_slot)
    return (
        front.reshape(parent_rows, 1, EXTENT, parent_cols, 1, 1, EXTENT),
        parent_factor.reshape(parent_lead_panel.shape),
        pivot,
    )


def solution(mesh):
    in_specs = (
        P("half", None, None),
        P("half", None, "row", None, None),
        P("half", None, "row", None, None, "col", None),
        P(),
        P(None, "row", "half", "col", None, None),
        P(),
    )
    out_specs = (
        P(None, "row", None, None, "half", "col", None),
        P(None, "row", "half", "col", None, None),
        P(),
    )
    return jax.shard_map(
        per_device, mesh=mesh, in_specs=in_specs, out_specs=out_specs, check_vma=False
    )
```
